32 devices in a mesh: dp: 8 (over z, x), seq: 4 (over y, core).
Axes of the slice: x: 2, y: 2, z: 4, core: 2. Of those that a mesh axis runs over, the one named last changes fastest.
Arguments:
- inputs: bfloat16 [16, 1024, 1152], P('dp', 'seq'), may hold values from -6 to 6
- segments: int32 [16, 1024], P('dp', 'seq'), may hold values from 0 to 4, as said below
- query_weight: bfloat16 [1152, 1024], P(None, ('dp', 'seq')), may hold values from -0.1875 to 0.1875
- key_weight: bfloat16 [1152, 256], P(None, ('dp', 'seq')), may hold values from -0.1875 to 0.1875
- value_weight: bfloat16 [1152, 256], P(None, ('dp', 'seq')), may hold values from -0.1875 to 0.1875
- out_weight: bfloat16 [1024, 1152], P(('dp', 'seq')), may hold values from -0.1875 to 0.1875
- gate_weight: bfloat16 [1152, 6912], P(None, ('dp', 'seq')), may hold values from -0.1875 to 0.1875
- up_weight: bfloat16 [1152, 6912], P(None, ('dp', 'seq')), may hold values from -0.1875 to 0.1875
- down_weight: bfloat16 [6912, 1152], P(('dp', 'seq')), may hold values from -0.078125 to 0.078125
- input_gain: float32 [1152], replicated, may hold values from -0.9 to 0.9
- attention_gain: float32 [1152], replicated, may hold values from -0.9 to 0.9
- feed_gain: float32 [1152], replicated, may hold values from -0.9 to 0.9
- output_gain: float32 [1152], replicated, may hold values from -0.9 to 0.9
- query_gain: float32 [256], replicated, may hold values from -0.9 to 0.9
- key_gain: float32 [256], replicated, may hold values from -0.9 to 0.9
- cotangent: bfloat16 [16, 1024, 1152], P('dp', 'seq'), may hold values from -6 to 6
Outputs:
- output: bfloat16 [16, 1024, 1152], P('dp', 'seq')
- grad_inputs: float32 [16, 1024, 1152], P('dp', 'seq')
- grad_query_weight: float32 [1152, 1024], P(None, ('dp', 'seq'))
- grad_key_weight: float32 [1152, 256], P(None, ('dp', 'seq'))
- grad_value_weight: float32 [1152, 256], P(None, ('dp', 'seq'))
- grad_out_weight: float32 [1024, 1152], P(('dp', 'seq'))
- grad_gate_weight: float32 [1152, 6912], P(None, ('dp', 'seq'))
- grad_up_weight: float32 [1152, 6912], P(None, ('dp', 'seq'))
- grad_down_weight: float32 [6912, 1152], P(('dp', 'seq'))
- grad_input_gain: float32 [1152], replicated
- grad_attention_gain: float32 [1152], replicated
- grad_feed_gain: float32 [1152], replicated
- grad_output_gain: float32 [1152], replicated
- grad_query_gain: float32 [256], replicated
- grad_key_gain: float32 [256], replicated
The draws below stay inside these ranges and needn't reach their ends.
Inputs may be any that keep to these rules, and one draw needn't show every extreme that they name: `segments`: in each sequence the ids start at 0 at the first token and rise by 0 or 1 from one token to the next, never above 4, which every draw reaches. Of the 2 sequences of each index of dp, one keeps a single id from token 128 to token 895.
All inputs are finite; a program needn't handle non-finite values.
Results may differ from the reference program's by a relative error of at most 0.017.
Values may be sent and summed in bfloat16 or wider, within the bound.
No kernel may reach another device: no remote copies, remote signals or barrier semaphores. Data moves between devices by JAX's collectives and lax.ppermute only.
A program may use at most 512 MiB of HBM per device.

```python
import jax
import jax.numpy as jnp
from jax import lax

D = 1152
HEADS = 4
HD = 256
FF = 6912
WINDOW = 512
SEQ_LEN = 1024
MICRO = 2
SEQS = 16
LEN_DEV = 256


def draw_segments(key, part):
    key = jax.random.fold_in(key, 11)
    flag_key, pick_key = jax.random.split(key)
    drawn = jax.random.randint(flag_key, (SEQS, SEQ_LEN), 0, 2 * LEN_DEV)
    starting = jnp.where(drawn == 0, 1, 0).astype(jnp.int32)
    columns = jnp.arange(SEQ_LEN, dtype=jnp.int32)[None, :]
    picked = jax.random.randint(pick_key, (SEQS // MICRO, 1), 0, MICRO)
    chosen = (jnp.arange(MICRO, dtype=jnp.int32)[None, :] == picked).reshape(SEQS, 1)
    half_block = LEN_DEV // 2
    ceiling = SEQ_LEN // LEN_DEV
    forced = (columns % half_block == 0) & (columns > 0) & (columns <= ceiling * half_block)
    starting = jnp.where(jnp.logical_not(chosen) & forced, 1, starting)
    middle = (columns >= LEN_DEV // 2) & (columns < SEQ_LEN - LEN_DEV // 2)
    starting = jnp.where(chosen & middle, 0, starting)
    starting = jnp.where(columns == 0, 0, starting)
    return jnp.minimum(jnp.cumsum(starting, axis=1), ceiling).astype(jnp.int32)


def shard_levels(rng, dims, shards, least, high):
    level = 1.0
    for axis_at, blocks in shards:
        draws = jax.random.uniform(jax.random.fold_in(jax.random.fold_in(rng, 6), axis_at), (blocks,), jnp.float32, least / len(shards), high / len(shards))
        level = level * jnp.repeat(jnp.exp(draws), dims[axis_at] // blocks).reshape((-1,) + (1,) * (len(dims) - 1 - axis_at))
    return level


def scatter_about(rng, dims, scale, limit, shards=(), kind=jnp.bfloat16):
    array = scale * jax.random.normal(rng, dims, jnp.float32)
    if shards:
        array = array * shard_levels(rng, dims, shards, -0.22, 0.18)
    return jnp.clip(array, -limit, limit).astype(kind)


def setup_inputs(seed: int = 0) -> dict:
    arg_keys = jax.random.split(jax.random.key(seed), 17)
    inputs = scatter_about(arg_keys[0], (SEQS, SEQ_LEN, D), 1.0, 6.0, ((0, 8), (1, 4)))
    segments = draw_segments(jax.random.fold_in(arg_keys[16], 71), 0)
    query_weight = scatter_about(arg_keys[2], (D, HEADS * HD), D ** -0.5, 0.1875, ((1, 32),))
    key_weight = scatter_about(arg_keys[3], (D, HD), D ** -0.5, 0.1875, ((1, 32),))
    value_weight = scatter_about(arg_keys[4], (D, HD), D ** -0.5, 0.1875, ((1, 32),))
    out_weight = scatter_about(arg_keys[5], (HEADS * HD, D), (HEADS * HD) ** -0.5, 0.1875, ((0, 32),))
    gate_weight = scatter_about(arg_keys[6], (D, FF), D ** -0.5, 0.1875, ((1, 32),))
    up_weight = scatter_about(arg_keys[7], (D, FF), D ** -0.5, 0.1875, ((1, 32),))
    down_weight = scatter_about(arg_keys[8], (FF, D), FF ** -0.5, 0.078125, ((0, 32),))
    input_gain = scatter_about(arg_keys[9], (D,), 0.3, 0.9, (), jnp.float32)
    attention_gain = scatter_about(arg_keys[10], (D,), 0.3, 0.9, (), jnp.float32)
    feed_gain = scatter_about(arg_keys[11], (D,), 0.3, 0.9, (), jnp.float32)
    output_gain = scatter_about(arg_keys[12], (D,), 0.3, 0.9, (), jnp.float32)
    query_gain = scatter_about(arg_keys[13], (HD,), 0.3, 0.9, (), jnp.float32)
    key_gain = scatter_about(arg_keys[14], (HD,), 0.3, 0.9, (), jnp.float32)
    cotangent = scatter_about(arg_keys[15], (SEQS, SEQ_LEN, D), 1.0, 6.0, ((0, 8), (1, 4)))
    return {"inputs": inputs, "segments": segments, "query_weight": query_weight, "key_weight": key_weight, "value_weight": value_weight, "out_weight": out_weight, "gate_weight": gate_weight, "up_weight": up_weight, "down_weight": down_weight, "input_gain": input_gain, "attention_gain": attention_gain, "feed_gain": feed_gain, "output_gain": output_gain, "query_gain": query_gain, "key_gain": key_gain, "cotangent": cotangent}


@jax.custom_vjp
def low(v):
    return lax.optimization_barrier(v.astype(jnp.bfloat16)).astype(jnp.float32)

@jax.custom_vjp
def low_back(v):
    return v

def low_keep(v):
    return (low(v), None)

def low_pass(kept, grad):
    return (grad,)

def back_keep(v):
    return (v, None)

def back_low(kept, grad):
    return (low(grad),)
low.defvjp(low_keep, low_pass)
low_back.defvjp(back_keep, back_low)
epsilon = 1e-06

def rms_scale(values, gain):
    mean_square = lax.optimization_barrier(jnp.mean(values * values, axis=-1, keepdims=True))
    return values * lax.rsqrt(mean_square + epsilon) * (1.0 + gain)

def matmul(left, right):
    return jnp.dot(left, right, precision=lax.Precision.HIGHEST, preferred_element_type=jnp.float32)

def rope_tables(positions, width):
    steps = jnp.arange(width // 2, dtype=jnp.float32)
    inverse = 10000.0 ** (-2.0 * steps / width)
    angles = positions.astype(jnp.float32)[:, None] * inverse[None, :]
    doubled = jnp.concatenate([angles, angles], axis=-1)
    return (jnp.cos(doubled), jnp.sin(doubled))

def rotate(values, cosine, sine):
    half = values.shape[-1] // 2
    turned = jnp.concatenate([-values[..., half:], values[..., :half]], axis=-1)
    return values * cosine + turned * sine

def layer(inputs, segment, query_weight, key_weight, value_weight, out_weight, gate_weight, up_weight, down_weight, input_gain, attention_gain, feed_gain, output_gain, query_gain, key_gain):
    length = inputs.shape[0]
    normed = low(rms_scale(inputs, input_gain))
    query_proj = low_back(matmul(normed, query_weight)).reshape(length, HEADS, HD)
    key_proj = low_back(matmul(normed, key_weight))
    value_low = low(low_back(matmul(normed, value_weight)))
    positions = jnp.arange(length)
    cosine, sine = rope_tables(positions, HD)
    query_rot = low(rotate(rms_scale(query_proj, query_gain), cosine[:, None, :], sine[:, None, :]))
    key_rot = low(rotate(rms_scale(key_proj, key_gain), cosine, sine))
    scale = 1.0 / jnp.sqrt(jnp.float32(HD))
    scores = low_back(jnp.einsum('qhd,kd->hqk', query_rot, key_rot, precision=lax.Precision.HIGHEST) * scale)
    allowed = (positions[None, :] <= positions[:, None]) & (positions[:, None] - positions[None, :] < WINDOW)
    allowed = allowed & (segment[:, None] == segment[None, :])
    masked = jnp.where(allowed[None], scores, -1e+30)
    highest = lax.optimization_barrier(jnp.max(masked, axis=-1, keepdims=True))
    expo = jnp.exp(masked - highest)
    probs = low(expo / lax.optimization_barrier(jnp.sum(expo, axis=-1, keepdims=True)))
    mixed = jnp.einsum('hqk,kd->qhd', probs, value_low, precision=lax.Precision.HIGHEST)
    mixed = low(low_back(mixed.reshape(length, HEADS * HD)))
    attended = low_back(matmul(mixed, out_weight))
    hidden = inputs + rms_scale(attended, attention_gain)
    prenorm = low(rms_scale(hidden, feed_gain))
    gate = low_back(matmul(prenorm, gate_weight))
    upward = low_back(matmul(prenorm, up_weight))
    product = low(jax.nn.gelu(gate, approximate=True) * upward)
    down = low_back(matmul(product, down_weight))
    return hidden + rms_scale(down, output_gain)

def reference(inputs, segments, query_weight, key_weight, value_weight, out_weight, gate_weight, up_weight, down_weight, input_gain, attention_gain, feed_gain, output_gain, query_gain, key_gain, cotangent):
    params = (query_weight.astype(jnp.float32), key_weight.astype(jnp.float32), value_weight.astype(jnp.float32), out_weight.astype(jnp.float32), gate_weight.astype(jnp.float32), up_weight.astype(jnp.float32), down_weight.astype(jnp.float32), input_gain, attention_gain, feed_gain, output_gain, query_gain, key_gain)

    def one_sequence(totals, item):
        seq_inputs, seq_segment, seq_cot = item

        def forward(seq_values, *weights):
            return layer(seq_values, seq_segment, *weights)
        result, pullback = jax.vjp(forward, seq_inputs.astype(jnp.float32), *params)
        grads = pullback(seq_cot.astype(jnp.float32))
        totals = tuple((total + grad for total, grad in zip(totals, grads[1:])))
        return (totals, (result.astype(jnp.bfloat16), grads[0]))
    start = tuple((jnp.zeros(param.shape, jnp.float32) for param in params))
    totals, (outputs, grad_inputs) = lax.scan(one_sequence, start, (inputs, segments, cotangent))
    return (outputs, grad_inputs, totals[0], totals[1], totals[2], totals[3], totals[4], totals[5], totals[6], totals[7], totals[8], totals[9], totals[10], totals[11], totals[12])
```

```python
import jax
import jax.numpy as jnp
from jax import lax
from jax.sharding import PartitionSpec as P

HEADS = 4
WINDOW = 512

epsilon = 1e-06
both = ("dp", "seq")
low = jnp.bfloat16
wide = jnp.float32


def flipped(value, bits):
    count = lax.axis_size("seq")
    return lax.ppermute(value, "seq", [(index, index ^ bits) for index in range(count)])


def passed_along(value, axis, steps):
    count = lax.axis_size(axis)
    leading, last = (max(0, -steps), min(count, count - steps))
    return lax.ppermute(value, axis, [(source, source + steps) for source in range(leading, last)])


def seq_gather(rows):
    across = flipped(rows, 2)
    return jnp.concatenate([flipped(rows, 1), flipped(across, 1), rows, across], axis=0)


def seq_reduce(partner, own):
    rows = own.shape[0] // 2
    summed = own + flipped(partner, 1).astype(wide)
    return summed[:rows] + flipped(summed[rows:].astype(low), 2).astype(wide)


def rms_parts(values):
    scale = lax.rsqrt(jnp.mean(values * values, axis=-1, keepdims=True) + epsilon)
    return values * scale, scale


def rms_back(unit, scale, gain, grad):
    weighted = grad * (1.0 + gain)
    inner = jnp.mean(unit * weighted, axis=-1, keepdims=True)
    axes = tuple(range(grad.ndim - 1))
    return scale * (weighted - unit * inner), jnp.sum(unit * grad, axis=axes)


def rope_tables(positions, width):
    steps = jnp.arange(width // 2, dtype=wide)
    inverse = 10000.0 ** (-2.0 * steps / width)
    angles = positions.astype(wide)[:, None] * inverse[None, :]
    doubled = jnp.concatenate([angles, angles], axis=-1)
    return (jnp.cos(doubled), jnp.sin(doubled))


def rotate(values, cosine, sine):
    half = values.shape[-1] // 2
    turned = jnp.concatenate([-values[..., half:], values[..., :half]], axis=-1)
    return values * cosine + turned * sine


def rotate_back(grad, cosine, sine):
    half = grad.shape[-1] // 2
    swung = grad * sine
    turned = jnp.concatenate([swung[..., half:], -swung[..., :half]], axis=-1)
    return grad * cosine + turned


def product_of(left, right, left_axis, right_axis):
    return lax.dot_general(
        left, right, (((left_axis,), (right_axis,)), ((), ())), preferred_element_type=wide
    )


def gelu_parts(gate):
    inner = 0.7978845608028654 * (gate + 0.044715 * gate * gate * gate)
    bend = jnp.tanh(inner)
    value = 0.5 * gate * (1.0 + bend)
    slope = 0.5 * (1.0 + bend) + 0.5 * gate * (1.0 - bend * bend) * 0.7978845608028654 * (
        1.0 + 3.0 * 0.044715 * gate * gate
    )
    return value, slope


def on_device(
    inputs,
    segments,
    query_weight,
    key_weight,
    value_weight,
    out_weight,
    gate_weight,
    up_weight,
    down_weight,
    input_gain,
    attention_gain,
    feed_gain,
    output_gain,
    query_gain,
    key_gain,
    cotangent,
):
    micro, length, width = inputs.shape
    rows = micro * length
    size = query_gain.shape[0]
    heads = HEADS
    scale = 1.0 / jnp.sqrt(wide(size))
    seq_count = lax.axis_size("seq")
    hops = min((WINDOW + length - 2) // length, seq_count - 1)
    seq_index = lax.axis_index("seq")
    nq, nk, nv = query_weight.shape[1], key_weight.shape[1], value_weight.shape[1]

    attn_shard = jnp.concatenate([query_weight.T, key_weight.T, value_weight.T, out_weight], axis=0)
    attn_all = lax.all_gather(attn_shard, both, axis=0, tiled=False)
    ends = (nq, nq + nk, nq + nk + nv)
    full_qkv = jnp.concatenate(
        [
            attn_all[:, : ends[0]].reshape(-1, width),
            attn_all[:, ends[0] : ends[1]].reshape(-1, width),
            attn_all[:, ends[1] : ends[2]].reshape(-1, width),
        ],
        axis=0,
    )
    full_out = attn_all[:, ends[2] :].reshape(-1, width)
    gate_all = lax.all_gather(gate_weight.T, "dp", axis=0, tiled=True)
    up_all = lax.all_gather(up_weight.T, "dp", axis=0, tiled=True)
    down_all = lax.all_gather(down_weight, "dp", axis=0, tiled=True)

    positions = seq_index * length + jnp.arange(length, dtype=jnp.int32)
    cosine, sine = rope_tables(positions, size)
    source = inputs.reshape(rows, width).astype(wide)
    source_unit, source_scale = rms_parts(source)
    normed = (source_unit * (1.0 + input_gain)).astype(low)
    projected = product_of(normed, full_qkv, 1, 1)
    hq = heads * size
    query_proj = projected[:, :hq].reshape(micro, length, heads, size)
    key_proj = projected[:, hq : hq + size].reshape(micro, length, size)
    value_low = projected[:, hq + size :].astype(low).reshape(micro, length, size)
    query_unit, query_scale = rms_parts(query_proj)
    key_unit, key_scale = rms_parts(key_proj)
    query_low = rotate(
        query_unit * (1.0 + query_gain), cosine[:, None, :], sine[:, None, :]
    ).astype(low)
    query_low = query_low.reshape(micro, length * heads, size)
    key_low = rotate(key_unit * (1.0 + key_gain), cosine, sine).astype(low)
    own_block = jnp.concatenate([key_low, value_low], axis=-1)
    blocks = [own_block]
    seg_blocks = [segments]
    for hop in range(1, hops + 1):
        blocks.insert(0, passed_along(own_block, "seq", hop))
        seg_blocks.insert(0, passed_along(segments, "seq", hop))
    all_keys = jnp.concatenate(blocks, axis=1)
    key_seg = jnp.concatenate(seg_blocks, axis=1)
    keys_only = all_keys[..., :size]
    values_only = all_keys[..., size:]
    key_count = (hops + 1) * length
    key_pos = seq_index * length - hops * length + jnp.arange(key_count, dtype=jnp.int32)
    query_pos = jnp.broadcast_to(positions[:, None], (length, heads)).reshape(length * heads)
    window = (key_pos[None, :] >= 0) & (key_pos[None, :] <= query_pos[:, None])
    window = window & (query_pos[:, None] - key_pos[None, :] < WINDOW)
    mixed, kept = [], []
    for item in range(micro):
        row_seg = jnp.broadcast_to(segments[item][:, None], (length, heads)).reshape(-1)
        allowed = window & (key_seg[item][None, :] == row_seg[:, None])
        scores = product_of(query_low[item], keys_only[item], 1, 1) * scale
        masked = jnp.where(allowed, scores, -1e30)
        highest = jnp.max(masked, axis=-1, keepdims=True)
        expo = jnp.exp(masked - highest)
        total = jnp.sum(expo, axis=-1, keepdims=True)
        probs = (expo / total).astype(low)
        mixed.append(product_of(probs, values_only[item], 1, 0).astype(low))
        kept.append((allowed, highest + jnp.log(total)))
    mixed_flat = jnp.stack(mixed).reshape(rows, hq)
    attended = product_of(mixed_flat, full_out, 1, 0)
    attended_unit, attended_scale = rms_parts(attended)
    hidden = source + attended_unit * (1.0 + attention_gain)
    hidden_unit, hidden_scale = rms_parts(hidden)
    prenorm = (hidden_unit * (1.0 + feed_gain)).astype(low)

    group = seq_gather(prenorm)
    half = 2 * rows
    gate = product_of(group, gate_all, 1, 1)
    upward = product_of(group, up_all, 1, 1)
    product = (gelu_parts(gate)[0] * upward).astype(low)
    down = seq_reduce(
        product_of(product[:half], down_all, 1, 0).astype(low),
        product_of(product[half:], down_all, 1, 0),
    )
    down_unit, down_scale = rms_parts(down)
    output = (hidden + down_unit * (1.0 + output_gain)).astype(low)

    grad_result = cotangent.reshape(rows, width).astype(wide)
    grad_down, grad_output_gain = rms_back(down_unit, down_scale, output_gain, grad_result)
    grad_group = seq_gather(grad_down.astype(low))
    grad_down_weight = product_of(product, grad_group, 0, 0).astype(low)
    shard_down = lax.psum_scatter(grad_down_weight, "dp", scatter_dimension=0, tiled=True)
    grad_product = product_of(grad_group, down_all, 1, 1)
    value, slope = gelu_parts(gate)
    grad_gate = (grad_product * upward * slope).astype(low)
    grad_up = (grad_product * value).astype(low)
    grad_prenorm = seq_reduce(
        (product_of(grad_gate[:half], gate_all, 1, 0) + product_of(grad_up[:half], up_all, 1, 0)).astype(low),
        product_of(grad_gate[half:], gate_all, 1, 0) + product_of(grad_up[half:], up_all, 1, 0),
    )
    grad_gate_weight = product_of(grad_gate, group, 0, 0).astype(low)
    shard_gate = lax.psum_scatter(grad_gate_weight, "dp", scatter_dimension=0, tiled=True)
    grad_up_weight = product_of(grad_up, group, 0, 0).astype(low)
    shard_up = lax.psum_scatter(grad_up_weight, "dp", scatter_dimension=0, tiled=True)

    grad_part, grad_feed_gain = rms_back(hidden_unit, hidden_scale, feed_gain, grad_prenorm)
    grad_hidden = grad_result + grad_part
    grad_attended, grad_attention_gain = rms_back(
        attended_unit, attended_scale, attention_gain, grad_hidden
    )
    grad_attended = grad_attended.astype(low)
    grad_out = product_of(mixed_flat, grad_attended, 0, 0).astype(low)
    grad_mixed = product_of(grad_attended, full_out, 1, 1).astype(low)
    grad_mixed = grad_mixed.reshape(micro, length * heads, size)
    grad_query_rows, key_grads = [], []
    for item in range(micro):
        allowed, log_total = kept[item]
        scores = product_of(query_low[item], keys_only[item], 1, 1) * scale
        probs = jnp.where(allowed, jnp.exp(scores - log_total), 0.0)
        grad_probs = product_of(grad_mixed[item], values_only[item], 1, 1)
        delta = jnp.sum(probs * grad_probs, axis=-1, keepdims=True)
        grad_scores = (probs * (grad_probs - delta)).astype(low)
        grad_query_rows.append(product_of(grad_scores, keys_only[item], 1, 0) * scale)
        grad_keys = product_of(grad_scores, query_low[item], 0, 0) * scale
        grad_values = product_of(probs.astype(low), grad_mixed[item], 0, 0)
        key_grads.append(jnp.concatenate([grad_keys, grad_values], axis=-1))
    key_grads = jnp.stack(key_grads)
    returning = key_grads[:, hops * length :]
    for hop in range(1, hops + 1):
        block = key_grads[:, (hops - hop) * length : (hops - hop + 1) * length]
        returning = returning + passed_along(block.astype(low), "seq", -hop).astype(wide)
    grad_query_rows = jnp.stack(grad_query_rows).reshape(micro, length, heads, size)
    grad_query_proj, grad_query_gain = rms_back(
        query_unit,
        query_scale,
        query_gain,
        rotate_back(grad_query_rows, cosine[:, None, :], sine[:, None, :]),
    )
    grad_key_proj, grad_key_gain = rms_back(
        key_unit, key_scale, key_gain, rotate_back(returning[..., :size], cosine, sine)
    )
    grad_projected = jnp.concatenate(
        [
            grad_query_proj.astype(low).reshape(rows, hq),
            grad_key_proj.astype(low).reshape(rows, size),
            returning[..., size:].astype(low).reshape(rows, size),
        ],
        axis=-1,
    )
    grad_qkv = product_of(grad_projected, normed, 0, 0).astype(low)
    grad_normed = product_of(grad_projected, full_qkv, 1, 0)
    grad_source, grad_input_gain = rms_back(source_unit, source_scale, input_gain, grad_normed)
    grad_inputs = grad_hidden + grad_source

    count = attn_all.shape[0]
    grad_attn = jnp.concatenate(
        [
            grad_qkv[:hq].reshape(count, nq, width),
            grad_qkv[hq : hq + size].reshape(count, nk, width),
            grad_qkv[hq + size :].reshape(count, nv, width),
            grad_out.reshape(count, -1, width),
        ],
        axis=1,
    )
    shard_attn = lax.psum_scatter(grad_attn, both, scatter_dimension=0, tiled=False).astype(wide)
    gains = lax.psum(
        jnp.concatenate(
            [
                grad_input_gain,
                grad_attention_gain,
                grad_feed_gain,
                grad_output_gain,
                grad_query_gain,
                grad_key_gain,
            ]
        ),
        both,
    )
    return (
        output.reshape(micro, length, width),
        grad_inputs.reshape(micro, length, width),
        shard_attn[: ends[0]].T,
        shard_attn[ends[0] : ends[1]].T,
        shard_attn[ends[1] : ends[2]].T,
        shard_attn[ends[2] :],
        shard_gate.astype(wide).T,
        shard_up.astype(wide).T,
        shard_down.astype(wide),
        gains[:width],
        gains[width : 2 * width],
        gains[2 * width : 3 * width],
        gains[3 * width : 4 * width],
        gains[4 * width : 4 * width + size],
        gains[4 * width + size :],
    )


def solution(mesh):
    in_specs = (
        P("dp", "seq", None),
        P("dp", "seq"),
        P(None, ("dp", "seq")),
        P(None, ("dp", "seq")),
        P(None, ("dp", "seq")),
        P(("dp", "seq"), None),
        P(None, ("dp", "seq")),
        P(None, ("dp", "seq")),
        P(("dp", "seq"), None),
        P(),
        P(),
        P(),
        P(),
        P(),
        P(),
        P("dp", "seq", None),
    )
    out_specs = (
        P("dp", "seq", None),
        P("dp", "seq", None),
        P(None, ("dp", "seq")),
        P(None, ("dp", "seq")),
        P(None, ("dp", "seq")),
        P(("dp", "seq"), None),
        P(None, ("dp", "seq")),
        P(None, ("dp", "seq")),
        P(("dp", "seq"), None),
        P(),
        P(),
        P(),
        P(),
        P(),
        P(),
    )
    return jax.shard_map(
        on_device, mesh=mesh, in_specs=in_specs, out_specs=out_specs, check_vma=False
    )
```

```python
import functools

import jax
import jax.numpy as jnp
from jax import lax
from jax.experimental import pallas as pl
from jax.experimental.pallas import tpu as pltpu
from jax.sharding import PartitionSpec as P

HEADS = 4
WINDOW = 512

epsilon = 1e-06
both = ("dp", "seq")
low = jnp.bfloat16
wide = jnp.float32


def flipped(value, bits):
    count = lax.axis_size("seq")
    return lax.ppermute(value, "seq", [(index, index ^ bits) for index in range(count)])


def passed_along(value, axis, steps):
    count = lax.axis_size(axis)
    leading, last = (max(0, -steps), min(count, count - steps))
    return lax.ppermute(value, axis, [(source, source + steps) for source in range(leading, last)])


def by_steps():
    return lax.axis_size("dp") == 8 and lax.axis_size("seq") == 4


def along_z(value, steps):
    return lax.ppermute(value, "dp", [(index, (index + 2 * steps) % 8) for index in range(8)])


def along_x(value):
    return lax.ppermute(value, "dp", [(index, index ^ 1) for index in range(8)])


def column_groups():
    return [[2 * z + x for z in range(4)] for x in range(2)] if by_steps() else None


def hidden_gather(shard):
    return lax.all_gather(shard, "dp", axis=0, axis_index_groups=column_groups(), tiled=True)


def hidden_reduce(terms):
    return lax.psum_scatter(
        terms.astype(low), "dp", scatter_dimension=0, axis_index_groups=column_groups(), tiled=True
    ).astype(wide)


def tied(*values):
    return lax.optimization_barrier(values)


def group_gather(rows):
    across_y = flipped(rows, 2)
    if by_steps():
        half = rows.shape[0] // 2
        across_x = along_x(rows)
        diagonal = jnp.concatenate([along_x(across_y[:half]), flipped(across_x[half:], 2)], axis=0)
        own = [diagonal, across_x, across_y, rows]
    else:
        own = [across_y, rows]
    return [flipped(block, 1) for block in own], own


def group_reduce(sent, kept, beside=lambda ready: None, last=lambda ready: None):
    got = flipped(sent, 1)
    rows = kept[0].shape[0]
    half = rows // 2
    part = lambda start, end: got[start:end].astype(wide)
    if not by_steps():
        crossing = (kept[0] + part(0, rows)).astype(low)
        return (kept[1], got[rows:], flipped(crossing, 2)), beside(sent), last(sent)
    diagonal = (kept[0] + part(0, rows)).astype(low)
    diagonal, got, *kept = tied(diagonal, got, *kept[1:])
    aside = beside(kept[0])
    for_y, for_x = along_x(diagonal[:half]), flipped(diagonal[half:], 2)
    for_y, for_x, aside, *kept = tied(for_y, for_x, aside, *kept)
    nothing = jnp.zeros_like(for_x, dtype=wide)
    x_part = kept[0] + part(rows, 2 * rows) + jnp.concatenate([nothing, for_x.astype(wide)], axis=0)
    y_part = kept[1] + part(2 * rows, 3 * rows) + jnp.concatenate([for_y.astype(wide), nothing], axis=0)
    x_part, y_part, *kept = tied(x_part.astype(low), y_part.astype(low), *kept)
    after = last(kept[-1])
    x_part, y_part, after = tied(along_x(x_part), flipped(y_part, 2), after)
    return (kept[-1], got[3 * rows :], x_part, y_part), aside, after


def reduce_step(terms, names, name):
    dp, seq = lax.axis_index("dp"), lax.axis_index("seq")
    own = {"x": dp % 2, "y": seq // 2, "core": seq % 2}[name]
    send = {"x": along_x, "y": lambda v: flipped(v, 2), "core": lambda v: flipped(v, 1)}[name]
    at = names.index(name)
    names.pop(at)
    kept = lax.dynamic_index_in_dim(terms, own, at, keepdims=False)
    sent = lax.dynamic_index_in_dim(terms, 1 - own, at, keepdims=False)
    return kept.astype(wide) + send(sent.astype(low)).astype(wide)


def reduce_first(terms):
    if not by_steps():
        return terms
    return reduce_step(terms.reshape(4, 2, 2, 2, *terms.shape[1:]), ["z", "x", "y", "core"], "core")


def reduce_rest(terms, order):
    if not by_steps():
        return lax.psum_scatter(terms.astype(low), both, scatter_dimension=0, tiled=False).astype(wide)
    z = lax.axis_index("dp") // 2
    names = ["z", "x", "y"]
    for name in order:
        terms = reduce_step(terms, names, name)
    total = lax.dynamic_index_in_dim(terms, z, 0, keepdims=False)
    for steps in (2, 1, 3):
        sent = lax.dynamic_index_in_dim(terms, (z - steps) % 4, 0, keepdims=False)
        total = total + along_z(sent.astype(low), -steps).astype(wide)
    return total


def sum_everywhere(values):
    if not by_steps():
        return lax.psum(values, both)
    values = values + flipped(values, 1)
    values = values + flipped(values, 2)
    values = values + along_x(values)
    values = values + along_z(values, 2)
    return values + along_z(values, 1)


def rms_parts(values):
    scale = lax.rsqrt(jnp.mean(values * values, axis=-1, keepdims=True) + epsilon)
    return values * scale, scale


def rms_back(unit, scale, gain, grad):
    weighted = grad * (1.0 + gain)
    inner = jnp.mean(unit * weighted, axis=-1, keepdims=True)
    axes = tuple(range(grad.ndim - 1))
    return scale * (weighted - unit * inner), jnp.sum(unit * grad, axis=axes)


def rope_tables(positions, width):
    steps = jnp.arange(width // 2, dtype=wide)
    inverse = 10000.0 ** (-2.0 * steps / width)
    angles = positions.astype(wide)[:, None] * inverse[None, :]
    doubled = jnp.concatenate([angles, angles], axis=-1)
    return (jnp.cos(doubled), jnp.sin(doubled))


def rotate(values, cosine, sine):
    half = values.shape[-1] // 2
    turned = jnp.concatenate([-values[..., half:], values[..., :half]], axis=-1)
    return values * cosine + turned * sine


def rotate_back(grad, cosine, sine):
    half = grad.shape[-1] // 2
    swung = grad * sine
    turned = jnp.concatenate([swung[..., half:], -swung[..., :half]], axis=-1)
    return grad * cosine + turned


def product_of(left, right, left_axis, right_axis):
    return lax.dot_general(
        left, right, (((left_axis,), (right_axis,)), ((), ())), preferred_element_type=wide
    )


def gelu_parts(gate):
    inner = 0.7978845608028654 * (gate + 0.044715 * gate * gate * gate)
    bend = jnp.tanh(inner)
    value = 0.5 * gate * (1.0 + bend)
    slope = 0.5 * (1.0 + bend) + 0.5 * gate * (1.0 - bend * bend) * 0.7978845608028654 * (
        1.0 + 3.0 * 0.044715 * gate * gate
    )
    return value, slope


def rms_back_rows(values, gain, grad):
    unit, scale = rms_parts(values)
    weighted = grad * (1.0 + gain)
    inner = jnp.mean(unit * weighted, axis=-1, keepdims=True)
    return unit, scale * (weighted - unit * inner), jnp.sum(unit * grad, axis=0, keepdims=True)


def total_of(terms):
    return functools.reduce(jnp.add, [term[...].astype(wide) for term in terms])


def turn_kernel(*refs):
    *terms, hidden, cotangent, gain, output, grad_down, grad_gain = refs
    down = total_of(terms)
    unit, grad, grad_gain[0] = rms_back_rows(down, gain[...], cotangent[...].astype(wide))
    output[...] = (hidden[...] + unit * (1.0 + gain[...])).astype(low)
    grad_down[...] = grad.astype(low)


def hidden_kernel(*refs):
    *terms, hidden, attended, cotangent, feed, attention, grad_hidden, grad_attended, gains = refs
    grad_prenorm = total_of(terms)
    _, grad, gains[0, 0:1] = rms_back_rows(hidden[...], feed[...], grad_prenorm)
    grad = grad + cotangent[...].astype(wide)
    grad_hidden[...] = grad
    _, grad, gains[0, 1:2] = rms_back_rows(attended[...], attention[...], grad)
    grad_attended[...] = grad.astype(low)


def by_rows(kernel, arrays, gains, kinds, gain_rows, tile=128):
    rows, width = arrays[-1].shape
    tiles = rows // tile
    block = pl.BlockSpec((tile, width), lambda item: (item, 0))
    gain_spec = pl.BlockSpec((1, width), lambda item: (0, 0))
    *results, grads = pl.pallas_call(
        kernel,
        grid=(tiles,),
        in_specs=[block] * len(arrays) + [gain_spec] * len(gains),
        out_specs=[block] * len(kinds) + [pl.BlockSpec((1, gain_rows, width), lambda item: (item, 0, 0))],
        out_shape=[jax.ShapeDtypeStruct((rows, width), kind) for kind in kinds]
        + [jax.ShapeDtypeStruct((tiles, gain_rows, width), wide)],
        compiler_params=pltpu.CompilerParams(vmem_limit_bytes=24 * 2**20),
        cost_estimate=pl.CostEstimate(
            flops=40 * rows * width, bytes_accessed=18 * rows * width, transcendentals=rows
        ),
    )(*arrays, *[gain.reshape(1, width) for gain in gains])
    return *results, jnp.sum(grads, axis=0)


def row_specs(blocks, tile):
    specs, starts, start = [], [], 0
    for block in blocks:
        count = block.shape[0] // tile
        specs.append(
            pl.BlockSpec(
                (tile, block.shape[1]),
                lambda item, start=start, count=count: (jnp.clip(item - start, 0, count - 1), 0),
            )
        )
        starts.append(start)
        start += count
    return specs, starts, start


def picked(refs, starts):
    item = pl.program_id(0)
    value = refs[0][...]
    for ref, start in zip(refs[1:], starts[1:]):
        value = jnp.where(item >= start, ref[...], value)
    return value


def put(refs, starts, value):
    item = pl.program_id(0)
    ends = [*starts[1:], pl.num_programs(0)]
    for ref, start, end in zip(refs, starts, ends):

        @pl.when((item >= start) & (item < end))
        def _():
            ref[...] = value.astype(ref.dtype)


def feed_kernel(counts, starts, *refs):
    ins, outs = counts
    blocks, (gate_all, up_all, down_all) = refs[:ins], refs[ins : ins + 3]
    rows, product, value, slope = refs[ins + 3 : ins + 7]
    rows[...] = picked(blocks, starts)
    gate = product_of(rows[...], gate_all[...], 1, 1)
    upward = product_of(rows[...], up_all[...], 1, 1)
    bent, bend_slope = gelu_parts(gate)
    mixed = (bent * upward).astype(low)
    product[...] = mixed
    value[...] = bent.astype(low)
    slope[...] = (bend_slope * upward).astype(low)
    put(refs[-outs:], starts if outs > 1 else [0], product_of(mixed, down_all[...], 1, 0))


def feed_back_kernel(counts, starts, *refs):
    ins, outs = counts
    blocks, (value, slope, gate_all, up_all, down_all) = refs[:ins], refs[ins : ins + 5]
    rows, grad_gate, grad_up = refs[ins + 5 : ins + 8]
    rows[...] = picked(blocks, starts)
    grad = product_of(rows[...], down_all[...], 1, 1)
    gate = (grad * slope[...].astype(wide)).astype(low)
    upward = (grad * value[...].astype(wide)).astype(low)
    grad_gate[...] = gate
    grad_up[...] = upward
    terms = product_of(gate, gate_all[...], 1, 0) + product_of(upward, up_all[...], 1, 0)
    put(refs[-outs:], starts if outs > 1 else [0], terms)


def feed(back, blocks, kept, weights, split):
    hidden, width = weights[0].shape
    tile = 512 if hidden <= 1024 else 256
    specs, starts, tiles = row_specs(blocks, tile)
    rows = tiles * tile
    inner = pl.BlockSpec((tile, hidden), lambda item: (item, 0))
    outer = pl.BlockSpec((tile, width), lambda item: (item, 0))
    full = pl.BlockSpec((hidden, width), lambda item: (0, 0), pipeline_mode=pl.Buffered(1))
    count = 2 if back else 3
    shape = jax.ShapeDtypeStruct
    if split:
        last_specs = specs
        last = [shape(block.shape, low) for block in blocks[:-1]] + [shape(blocks[-1].shape, wide)]
    else:
        last_specs, last = [outer], [shape((rows, width), low)]
    group, *results = pl.pallas_call(
        functools.partial(feed_back_kernel if back else feed_kernel, (len(blocks), len(last)), starts),
        grid=(tiles,),
        in_specs=specs + [inner] * len(kept) + [full] * 3,
        out_specs=[outer] + [inner] * count + last_specs,
        out_shape=[shape((rows, width), low)] + [shape((rows, hidden), low)] * count + last,
        compiler_params=pltpu.CompilerParams(vmem_limit_bytes=56 * 2**20),
        cost_estimate=pl.CostEstimate(
            flops=6 * rows * hidden * width,
            bytes_accessed=rows * (10 * hidden + 8 * width) + 6 * hidden * width,
            transcendentals=0 if back else rows * hidden,
        ),
    )(*blocks, *kept, *weights)
    return group, results[:count], results[count:] if split else results[count]


def weight_grad(lefts, rights):
    terms = [product_of(left, right, 0, 0) for left, right in zip(lefts, rights)]
    return (terms[0] + terms[1]).astype(low)


def weights_kernel(rows, place, *refs):
    blocks, outs = refs[:8], refs[8:]
    relative = pl.program_id(0) ^ place[0]
    for number, block in enumerate(blocks):

        @pl.when(relative == number)
        def _():
            for z in range(4):
                source = lax.rem(place[1] + 4 - z, 4)
                start = 0
                for out, count in zip(outs, rows):
                    out[z, 0] = block[source, start : start + count]
                    start += count


def attention_weights(shards):
    rows = [shard.shape[0] for shard in shards]
    width = shards[0].shape[1]
    shard = jnp.concatenate(shards, axis=0)
    if not by_steps():
        whole = lax.all_gather(shard, both, axis=0, tiled=False)
        starts = [sum(rows[:at]) for at in range(len(rows))]
        return [
            whole[:, start : start + count].reshape(-1, width) for start, count in zip(starts, rows)
        ]
    first, third, second = along_z(shard, 1), along_z(shard, 3), along_z(shard, 2)
    column = jnp.concatenate([shard, first, second, third], axis=0)
    far, near = group_gather(column)
    blocks = [block.reshape(4, -1, width) for at in (3, 2, 1, 0) for block in (near[at], far[at])]
    dp, seq = lax.axis_index("dp"), lax.axis_index("seq")
    place = jnp.stack([(dp % 2) * 4 + seq, dp // 2]).astype(jnp.int32)
    results = pl.pallas_call(
        functools.partial(weights_kernel, rows),
        grid=(8,),
        in_specs=[pl.BlockSpec(memory_space=pltpu.SMEM)]
        + [pl.BlockSpec((4, sum(rows), width), lambda item: (0, 0, 0), pipeline_mode=pl.Buffered(1))] * 8,
        out_specs=[pl.BlockSpec((4, 1, count, width), lambda item: (0, item, 0, 0)) for count in rows],
        out_shape=[jax.ShapeDtypeStruct((4, 8, count, width), shard.dtype) for count in rows],
        compiler_params=pltpu.CompilerParams(vmem_limit_bytes=24 * 2**20),
        cost_estimate=pl.CostEstimate(
            flops=0, bytes_accessed=64 * sum(rows) * width * 2, transcendentals=0
        ),
    )(place, *blocks)
    return [result.reshape(-1, width) for result in results]


def allowed_pairs(base, row_seg, column_seg, length, before):
    shape = (before + length, length)
    key = lax.broadcasted_iota(jnp.int32, shape, 0)
    distance = lax.broadcasted_iota(jnp.int32, shape, 1) + before - key
    allowed = (distance >= 0) & (distance < WINDOW) & (key >= before - base)
    return allowed & (column_seg == row_seg)


def shaped_query(projected, gain, cosine, sine):
    unit, scale = rms_parts(projected)
    return unit, scale, rotate(unit * (1.0 + gain), cosine, sine).astype(low)


def attend_kernel(heads, base, proj, cosine, sine, gain, own_seg, key_seg, *refs):
    *blocks, mixed, logs = refs
    length, size = cosine.shape
    keys = jnp.concatenate([block[0] for block in blocks], axis=0)
    only, values = keys[:, :size], keys[:, size:]
    before = keys.shape[0] - length
    allowed = allowed_pairs(base[0], own_seg[0], key_seg[0], length, before)
    for head in range(heads):
        at = slice(head * size, (head + 1) * size)
        _, _, query = shaped_query(proj[:, at], gain[...], cosine[...], sine[...])
        scores = product_of(only, query, 1, 1) * size**-0.5
        scores = jnp.where(allowed, scores, -1e30)
        highest = jnp.max(scores, axis=0, keepdims=True)
        expo = jnp.exp(scores - highest)
        total = jnp.sum(expo, axis=0, keepdims=True)
        probs = (expo * (1.0 / total)).astype(low)
        mixed[:, at] = product_of(probs.T, values, 1, 0).astype(low)
        logs[0, head : head + 1, :] = highest + jnp.log(total)


def attend_back_kernel(heads, base, proj, cosine, sine, gain, own_seg, key_seg, logs, grad, *refs):
    hops = (len(refs) - 3) // 2
    blocks, outs = refs[: hops + 1], refs[hops + 1 :]
    grad_proj, grad_gain = outs[0], outs[1]
    length, size = cosine.shape
    keys = jnp.concatenate([block[0] for block in blocks], axis=0)
    only, values = keys[:, :size], keys[:, size:]
    before = hops * length
    allowed = allowed_pairs(base[0], own_seg[0], key_seg[0], length, before)
    grad_keys = jnp.zeros((before + length, size), wide)
    grad_values = jnp.zeros((before + length, size), wide)
    gains = jnp.zeros((1, size), wide)
    for head in range(heads):
        at = slice(head * size, (head + 1) * size)
        unit, scale, query = shaped_query(proj[:, at], gain[...], cosine[...], sine[...])
        mixed_grad = grad[:, at]
        scores = product_of(only, query, 1, 1) * size**-0.5
        probs = jnp.where(allowed, jnp.exp(scores - logs[0, head : head + 1, :]), 0.0)
        grad_probs = product_of(values, mixed_grad, 1, 1)
        delta = jnp.sum(probs * grad_probs, axis=0, keepdims=True)
        grad_scores = (probs * (grad_probs - delta)).astype(low)
        grad_values += product_of(probs.astype(low), mixed_grad, 1, 0)
        grad_keys += product_of(grad_scores, query, 1, 0)
        grad_query = product_of(grad_scores.T, only, 1, 0) * size**-0.5
        turned = rotate_back(grad_query, cosine[...], sine[...])
        weighted = turned * (1.0 + gain[...])
        inner = jnp.mean(unit * weighted, axis=-1, keepdims=True)
        grad_proj[:, at] = (scale * (weighted - unit * inner)).astype(low)
        gains += jnp.sum(unit * turned, axis=0, keepdims=True)
    grad_gain[0] = gains
    for hop in range(hops + 1):
        rows = slice(hop * length, (hop + 1) * length)
        target = outs[2 + hop]
        target[0, :, :size] = (grad_keys[rows] * size**-0.5).astype(target.dtype)
        target[0, :, size:] = grad_values[rows].astype(target.dtype)


def attention(back, micro, length, base, projected, tables, gain, segments, key_seg, blocks, extra=()):
    size = gain.shape[-1]
    hops = len(blocks) - 1
    whole = lambda *shape: pl.BlockSpec(shape, lambda item: (0,) * len(shape))
    each = lambda *shape: pl.BlockSpec((1, *shape), lambda item: (item, 0, 0))
    flat = pl.BlockSpec((length, HEADS * size), lambda item: (item, 0))
    key_count = (hops + 1) * length
    in_specs = [
        pl.BlockSpec(memory_space=pltpu.SMEM),
        flat,
        whole(length, size),
        whole(length, size),
        whole(1, size),
        each(1, length),
        each(key_count, 1),
    ]
    logs_spec, block_spec = each(HEADS, length), each(length, 2 * size)
    shape = jax.ShapeDtypeStruct
    rows = (micro * length, HEADS * size)
    if back:
        in_specs += [logs_spec, flat]
        out_specs = [flat, each(1, size)] + [block_spec] * (hops + 1)
        out_shape = [shape(rows, low), shape((micro, 1, size), wide)]
        out_shape += [shape((micro, length, 2 * size), low)] * hops
        out_shape += [shape((micro, length, 2 * size), wide)]
    else:
        out_specs = [flat, logs_spec]
        out_shape = [shape(rows, low), shape((micro, HEADS, length), wide)]
    flops = micro * HEADS * key_count * length * size * 2 * (5 if back else 2)
    return pl.pallas_call(
        functools.partial(attend_back_kernel if back else attend_kernel, HEADS),
        grid=(micro,),
        in_specs=in_specs + [block_spec] * (hops + 1),
        out_specs=out_specs,
        out_shape=out_shape,
        compiler_params=pltpu.CompilerParams(vmem_limit_bytes=40 * 2**20),
        cost_estimate=pl.CostEstimate(
            flops=flops, bytes_accessed=10 * 2**20, transcendentals=micro * HEADS * key_count * length
        ),
    )(
        base.reshape(1),
        projected,
        *tables,
        gain.reshape(1, size),
        segments.reshape(micro, 1, length),
        key_seg.reshape(micro, key_count, 1),
        *extra,
        *blocks,
    )


def on_device(
    inputs,
    segments,
    query_weight,
    key_weight,
    value_weight,
    out_weight,
    gate_weight,
    up_weight,
    down_weight,
    input_gain,
    attention_gain,
    feed_gain,
    output_gain,
    query_gain,
    key_gain,
    cotangent,
):
    micro, length, width = inputs.shape
    rows = micro * length
    size = query_gain.shape[0]
    seq_count = lax.axis_size("seq")
    dp_count = lax.axis_size("dp")
    hops = min((WINDOW + length - 2) // length, seq_count - 1)
    seq_index = lax.axis_index("seq")
    nq, nk, nv = query_weight.shape[1], key_weight.shape[1], value_weight.shape[1]

    full_query, full_key, full_value, full_out = attention_weights(
        [query_weight.T, key_weight.T, value_weight.T, out_weight]
    )
    units = gate_weight.shape[1]
    shards = 4 if by_steps() else dp_count
    padding = next(extra for extra in range(129) if (units + extra) * shards % 128 == 0)
    padded = lambda shard: jnp.pad(shard, ((0, padding), (0, 0)))
    gate_all = hidden_gather(padded(gate_weight.T))
    up_all = hidden_gather(padded(up_weight.T))
    down_all = hidden_gather(padded(down_weight))

    positions = seq_index * length + jnp.arange(length, dtype=jnp.int32)
    cosine, sine = rope_tables(positions, size)
    source = inputs.reshape(rows, width).astype(wide)
    source_unit, source_scale = rms_parts(source)
    normed = (source_unit * (1.0 + input_gain)).astype(low)
    key_proj = product_of(normed, full_key, 1, 1).reshape(micro, length, size)
    value_low = product_of(normed, full_value, 1, 1).astype(low).reshape(micro, length, size)
    key_unit, key_scale = rms_parts(key_proj)
    key_low = rotate(key_unit * (1.0 + key_gain), cosine, sine).astype(low)
    own_block = jnp.concatenate([key_low, value_low], axis=-1)
    blocks = [own_block]
    seg_blocks = [segments]
    for hop in range(1, hops + 1):
        blocks.insert(0, passed_along(own_block, "seq", hop))
        seg_blocks.insert(0, passed_along(segments, "seq", hop))
    key_seg = jnp.concatenate(seg_blocks, axis=1)
    query_proj = product_of(normed, full_query, 1, 1)
    base = seq_index * length
    attend = functools.partial(
        attention,
        micro=micro,
        length=length,
        base=base,
        projected=query_proj,
        tables=(cosine, sine),
        gain=query_gain,
        segments=segments,
        key_seg=key_seg,
        blocks=blocks,
    )
    mixed_flat, logs = attend(back=False)
    attended = product_of(mixed_flat, full_out, 1, 0)
    attended_unit, attended_scale = rms_parts(attended)
    hidden = source + attended_unit * (1.0 + attention_gain)
    hidden_unit, hidden_scale = rms_parts(hidden)
    prenorm = (hidden_unit * (1.0 + feed_gain)).astype(low)

    weights = (gate_all, up_all, down_all)
    far, near = group_gather(prenorm)
    far, far_kept, sent = feed(False, far, (), weights, False)
    near, near_kept, kept = feed(False, near, (), weights, True)
    down, _, _ = group_reduce(sent, kept)
    flat_cotangent = cotangent.reshape(rows, width)
    output, grad_down, grad_output_gain = by_rows(
        turn_kernel, (*down, hidden, flat_cotangent), (output_gain,), (low, low), 1
    )

    grad_far, grad_near = group_gather(grad_down)
    grad_far, (far_gate, far_up), sent = feed(True, grad_far, far_kept[1:], weights, False)
    grad_near, (near_gate, near_up), kept = feed(True, grad_near, near_kept[1:], weights, True)

    def down_weight_grad(ready):
        left, _ = tied(near_kept[0], ready)
        return weight_grad((far_kept[0], left), (grad_far, grad_near))

    def gate_weight_grad(ready):
        left, _ = tied(near_gate, ready)
        return weight_grad((far_gate, left), (far, near))

    grad_prenorm, grad_down_weight, grad_gate_weight = group_reduce(
        sent, kept, down_weight_grad, gate_weight_grad
    )
    shard_down = hidden_reduce(grad_down_weight)[:units]
    shard_gate = hidden_reduce(grad_gate_weight)[:units]

    grad_hidden, grad_attended, gains = by_rows(
        hidden_kernel,
        (*grad_prenorm, hidden, attended, flat_cotangent),
        (feed_gain, attention_gain),
        (wide, low),
        2,
    )
    grad_feed_gain, grad_attention_gain = gains[0], gains[1]
    grad_out = product_of(mixed_flat, grad_attended, 0, 0).astype(low)
    grad_mixed = product_of(grad_attended, full_out, 1, 1).astype(low)
    grad_query_proj, query_gains, *key_grads = attend(back=True, extra=(logs, grad_mixed))
    grad_query_gain = jnp.sum(query_gains, axis=(0, 1))
    count = dp_count * seq_count
    grad_out = reduce_first(grad_out.reshape(count, -1, width))
    grad_query = product_of(grad_query_proj, normed, 0, 0).astype(low)
    grad_query = reduce_first(grad_query.reshape(count, nq, width))
    left, _ = tied(near_up, key_grads[hops])
    grad_up_weight = weight_grad((far_up, left), (far, near))
    shard_up = hidden_reduce(grad_up_weight)[:units]
    returning = key_grads[hops]
    for hop in range(1, hops + 1):
        returning = returning + passed_along(key_grads[hops - hop], "seq", -hop).astype(wide)
    returning, grad_out, grad_query, _ = tied(returning, grad_out, grad_query, grad_up_weight)
    shard_out = reduce_rest(grad_out, ("x", "y"))
    shard_query = reduce_rest(grad_query, ("y", "x"))
    grad_key_proj, grad_key_gain = rms_back(
        key_unit, key_scale, key_gain, rotate_back(returning[..., :size], cosine, sine)
    )
    grad_key = grad_key_proj.astype(low).reshape(rows, size)
    grad_value = returning[..., size:].astype(low).reshape(rows, size)
    grad_kv = [
        product_of(grad, normed, 0, 0).astype(low).reshape(count, -1, width)
        for grad in (grad_key, grad_value)
    ]
    grad_normed = product_of(grad_query_proj, full_query, 1, 0) + product_of(grad_key, full_key, 1, 0)
    grad_normed = grad_normed + product_of(grad_value, full_value, 1, 0)
    grad_source, grad_input_gain = rms_back(source_unit, source_scale, input_gain, grad_normed)
    grad_inputs = grad_hidden + grad_source

    shard_second = reduce_rest(reduce_first(jnp.concatenate(grad_kv, axis=1)), ("y", "x"))
    gains = sum_everywhere(
        jnp.concatenate(
            [
                grad_input_gain,
                grad_attention_gain,
                grad_feed_gain,
                grad_output_gain[0],
                grad_query_gain,
                grad_key_gain,
            ]
        )
    )
    return (
        output.reshape(micro, length, width),
        grad_inputs.reshape(micro, length, width),
        shard_query.T,
        shard_second[:nk].T,
        shard_second[nk:].T,
        shard_out,
        shard_gate.T,
        shard_up.T,
        shard_down,
        gains[:width],
        gains[width : 2 * width],
        gains[2 * width : 3 * width],
        gains[3 * width : 4 * width],
        gains[4 * width : 4 * width + size],
        gains[4 * width + size :],
    )


def solution(mesh):
    in_specs = (
        P("dp", "seq", None),
        P("dp", "seq"),
        P(None, ("dp", "seq")),
        P(None, ("dp", "seq")),
        P(None, ("dp", "seq")),
        P(("dp", "seq"), None),
        P(None, ("dp", "seq")),
        P(None, ("dp", "seq")),
        P(("dp", "seq"), None),
        P(),
        P(),
        P(),
        P(),
        P(),
        P(),
        P("dp", "seq", None),
    )
    out_specs = (
        P("dp", "seq", None),
        P("dp", "seq", None),
        P(None, ("dp", "seq")),
        P(None, ("dp", "seq")),
        P(None, ("dp", "seq")),
        P(("dp", "seq"), None),
        P(None, ("dp", "seq")),
        P(None, ("dp", "seq")),
        P(("dp", "seq"), None),
        P(),
        P(),
        P(),
        P(),
        P(),
        P(),
    )
    return jax.shard_map(
        on_device, mesh=mesh, in_specs=in_specs, out_specs=out_specs, check_vma=False
    )
```

```python
import functools

import jax
import jax.numpy as jnp
from jax import lax
from jax.experimental import pallas as pl
from jax.experimental.pallas import tpu as pltpu
from jax.sharding import PartitionSpec as P

HEADS = 4
WINDOW = 512

epsilon = 1e-06
both = ("dp", "seq")
low = jnp.bfloat16
wide = jnp.float32


def flipped(value, bits):
    count = lax.axis_size("seq")
    return lax.ppermute(value, "seq", [(index, index ^ bits) for index in range(count)])


def passed_along(value, axis, steps):
    count = lax.axis_size(axis)
    leading, last = (max(0, -steps), min(count, count - steps))
    return lax.ppermute(value, axis, [(source, source + steps) for source in range(leading, last)])


def by_steps():
    return lax.axis_size("dp") == 8 and lax.axis_size("seq") == 4


def along_z(value, steps):
    return lax.ppermute(value, "dp", [(index, (index + 2 * steps) % 8) for index in range(8)])


def along_x(value):
    return lax.ppermute(value, "dp", [(index, index ^ 1) for index in range(8)])


def column_groups():
    return [[2 * z + x for z in range(4)] for x in range(2)] if by_steps() else None


def hidden_gather(shard):
    return lax.all_gather(shard, "dp", axis=0, axis_index_groups=column_groups(), tiled=True)


def hidden_reduce(terms):
    return lax.psum_scatter(
        terms.astype(low), "dp", scatter_dimension=0, axis_index_groups=column_groups(), tiled=True
    ).astype(wide)


def tied(*values):
    return lax.optimization_barrier(values)


def group_gather(rows):
    across_y = flipped(rows, 2)
    if by_steps():
        half = rows.shape[0] // 2
        across_x = along_x(rows)
        diagonal = jnp.concatenate([along_x(across_y[:half]), flipped(across_x[half:], 2)], axis=0)
        own = [diagonal, across_x, across_y, rows]
    else:
        own = [across_y, rows]
    return [flipped(block, 1) for block in own], own


def group_reduce(sent, kept, beside=lambda ready: None, last=()):
    got = flipped(sent, 1)
    rows = kept[0].shape[0]
    half = rows // 2
    part = lambda start, end: got[start:end].astype(wide)
    if not by_steps():
        crossing = (kept[0] + part(0, rows)).astype(low)
        return (kept[1], got[rows:], flipped(crossing, 2)), beside(sent), [step(sent) for step in last]
    diagonal = (kept[0] + part(0, rows)).astype(low)
    diagonal, got, *kept = tied(diagonal, got, *kept[1:])
    aside = beside(kept[0])
    for_y, for_x = along_x(diagonal[:half]), flipped(diagonal[half:], 2)
    for_y, for_x, aside, *kept = tied(for_y, for_x, aside, *kept)
    nothing = jnp.zeros_like(for_x, dtype=wide)
    x_part = kept[0] + part(rows, 2 * rows) + jnp.concatenate([nothing, for_x.astype(wide)], axis=0)
    y_part = kept[1] + part(2 * rows, 3 * rows) + jnp.concatenate([for_y.astype(wide), nothing], axis=0)
    x_part, y_part, *kept = tied(x_part.astype(low), y_part.astype(low), *kept)
    if not last:
        return (kept[-1], got[3 * rows :], along_x(x_part), flipped(y_part, 2)), aside, ()
    first, second = last
    early = (along_x(x_part[:half]), flipped(y_part[:half], 2))
    first = first(kept[-1])
    early, first = tied(early, first)
    late = (along_x(x_part[half:]), flipped(y_part[half:], 2))
    second = second(early[0])
    late, second = tied(late, second)
    x_part, y_part = (jnp.concatenate(halves, axis=0) for halves in zip(early, late))
    return (kept[-1], got[3 * rows :], x_part, y_part), aside, (first, second)


def reduce_step(terms, names, name):
    dp, seq = lax.axis_index("dp"), lax.axis_index("seq")
    own = {"x": dp % 2, "y": seq // 2, "core": seq % 2}[name]
    send = {"x": along_x, "y": lambda v: flipped(v, 2), "core": lambda v: flipped(v, 1)}[name]
    at = names.index(name)
    names.pop(at)
    kept = lax.dynamic_index_in_dim(terms, own, at, keepdims=False)
    sent = lax.dynamic_index_in_dim(terms, 1 - own, at, keepdims=False)
    return kept.astype(wide) + send(sent.astype(low)).astype(wide)


def reduce_z(terms):
    z = lax.axis_index("dp") // 2
    total = lax.dynamic_index_in_dim(terms, z, 0, keepdims=False)
    for steps in (2, 1, 3):
        sent = lax.dynamic_index_in_dim(terms, (z - steps) % 4, 0, keepdims=False)
        total = total + along_z(sent.astype(low), -steps).astype(wide)
    return total


def sum_everywhere(values):
    if not by_steps():
        return lax.psum(values, both)
    values = (values + flipped(values, 1)) + (flipped(values, 2) + flipped(values, 3))
    values = values + along_x(values)
    return (values + along_z(values, 2)) + (along_z(values, 1) + along_z(values, 3))


def rms_parts(values):
    scale = lax.rsqrt(jnp.mean(values * values, axis=-1, keepdims=True) + epsilon)
    return values * scale, scale


def rms_back(unit, scale, gain, grad):
    weighted = grad * (1.0 + gain)
    inner = jnp.mean(unit * weighted, axis=-1, keepdims=True)
    axes = tuple(range(grad.ndim - 1))
    return scale * (weighted - unit * inner), jnp.sum(unit * grad, axis=axes)


def rope_tables(positions, width):
    steps = jnp.arange(width // 2, dtype=wide)
    inverse = 10000.0 ** (-2.0 * steps / width)
    angles = positions.astype(wide)[:, None] * inverse[None, :]
    doubled = jnp.concatenate([angles, angles], axis=-1)
    return (jnp.cos(doubled), jnp.sin(doubled))


def rotate(values, cosine, sine):
    half = values.shape[-1] // 2
    turned = jnp.concatenate([-values[..., half:], values[..., :half]], axis=-1)
    return values * cosine + turned * sine


def rotate_back(grad, cosine, sine):
    half = grad.shape[-1] // 2
    swung = grad * sine
    turned = jnp.concatenate([swung[..., half:], -swung[..., :half]], axis=-1)
    return grad * cosine + turned


def product_of(left, right, left_axis, right_axis):
    return lax.dot_general(
        left, right, (((left_axis,), (right_axis,)), ((), ())), preferred_element_type=wide
    )


def gelu_parts(gate):
    inner = 0.7978845608028654 * (gate + 0.044715 * gate * gate * gate)
    bend = jnp.tanh(inner)
    value = 0.5 * gate * (1.0 + bend)
    slope = 0.5 * (1.0 + bend) + 0.5 * gate * (1.0 - bend * bend) * 0.7978845608028654 * (
        1.0 + 3.0 * 0.044715 * gate * gate
    )
    return value, slope


def rms_back_rows(values, gain, grad):
    unit, scale = rms_parts(values)
    weighted = grad * (1.0 + gain)
    inner = jnp.mean(unit * weighted, axis=-1, keepdims=True)
    return unit, scale * (weighted - unit * inner), jnp.sum(unit * grad, axis=0, keepdims=True)


def total_of(terms):
    return functools.reduce(jnp.add, [term[...].astype(wide) for term in terms])


def turn_kernel(*refs):
    *terms, hidden, cotangent, gain, output, grad_down, grad_gain = refs
    down = total_of(terms)
    unit, grad, grad_gain[0] = rms_back_rows(down, gain[...], cotangent[...].astype(wide))
    output[...] = (hidden[...] + unit * (1.0 + gain[...])).astype(low)
    grad_down[...] = grad.astype(low)


def hidden_kernel(*refs):
    *terms, hidden, attended, cotangent, feed, attention, grad_hidden, grad_attended, gains = refs
    grad_prenorm = total_of(terms)
    _, grad, gains[0, 0:1] = rms_back_rows(hidden[...], feed[...], grad_prenorm)
    grad = grad + cotangent[...].astype(wide)
    grad_hidden[...] = grad
    _, grad, gains[0, 1:2] = rms_back_rows(attended[...], attention[...], grad)
    grad_attended[...] = grad.astype(low)


def by_rows(kernel, arrays, gains, kinds, gain_rows, tile=128):
    rows, width = arrays[-1].shape
    tiles = rows // tile
    block = pl.BlockSpec((tile, width), lambda item: (item, 0))
    gain_spec = pl.BlockSpec((1, width), lambda item: (0, 0))
    *results, grads = pl.pallas_call(
        kernel,
        grid=(tiles,),
        in_specs=[block] * len(arrays) + [gain_spec] * len(gains),
        out_specs=[block] * len(kinds) + [pl.BlockSpec((1, gain_rows, width), lambda item: (item, 0, 0))],
        out_shape=[jax.ShapeDtypeStruct((rows, width), kind) for kind in kinds]
        + [jax.ShapeDtypeStruct((tiles, gain_rows, width), wide)],
        compiler_params=pltpu.CompilerParams(vmem_limit_bytes=24 * 2**20),
        cost_estimate=pl.CostEstimate(
            flops=40 * rows * width, bytes_accessed=18 * rows * width, transcendentals=rows
        ),
    )(*arrays, *[gain.reshape(1, width) for gain in gains])
    return *results, jnp.sum(grads, axis=0)


def row_specs(blocks, tile):
    specs, starts, start = [], [], 0
    for block in blocks:
        count = block.shape[0] // tile
        specs.append(
            pl.BlockSpec(
                (tile, block.shape[1]),
                lambda item, start=start, count=count: (jnp.clip(item - start, 0, count - 1), 0),
            )
        )
        starts.append(start)
        start += count
    return specs, starts, start


def picked(refs, starts):
    item = pl.program_id(0)
    value = refs[0][...]
    for ref, start in zip(refs[1:], starts[1:]):
        value = jnp.where(item >= start, ref[...], value)
    return value


def put(refs, starts, value):
    item = pl.program_id(0)
    ends = [*starts[1:], pl.num_programs(0)]
    for ref, start, end in zip(refs, starts, ends):

        @pl.when((item >= start) & (item < end))
        def _():
            ref[...] = value.astype(ref.dtype)


def feed_kernel(counts, starts, *refs):
    ins, outs = counts
    blocks, (gate_all, up_all, down_all) = refs[:ins], refs[ins : ins + 3]
    rows, product, value, slope = refs[ins + 3 : ins + 7]
    rows[...] = picked(blocks, starts)
    gate = product_of(rows[...], gate_all[...], 1, 1)
    upward = product_of(rows[...], up_all[...], 1, 1)
    bent, bend_slope = gelu_parts(gate)
    mixed = (bent * upward).astype(low)
    product[...] = mixed
    value[...] = bent.astype(low)
    slope[...] = (bend_slope * upward).astype(low)
    put(refs[-outs:], starts if outs > 1 else [0], product_of(mixed, down_all[...], 1, 0))


def feed_back_kernel(counts, starts, *refs):
    ins, outs = counts
    blocks, (value, slope, gate_all, up_all, down_all) = refs[:ins], refs[ins : ins + 5]
    rows, grad_gate, grad_up = refs[ins + 5 : ins + 8]
    rows[...] = picked(blocks, starts)
    grad = product_of(rows[...], down_all[...], 1, 1)
    gate = (grad * slope[...].astype(wide)).astype(low)
    upward = (grad * value[...].astype(wide)).astype(low)
    grad_gate[...] = gate
    grad_up[...] = upward
    terms = product_of(gate, gate_all[...], 1, 0) + product_of(upward, up_all[...], 1, 0)
    put(refs[-outs:], starts if outs > 1 else [0], terms)


def feed(back, blocks, kept, weights, split):
    hidden, width = weights[0].shape
    tile = 512 if hidden <= 1024 else 256
    specs, starts, tiles = row_specs(blocks, tile)
    rows = tiles * tile
    inner = pl.BlockSpec((tile, hidden), lambda item: (item, 0))
    outer = pl.BlockSpec((tile, width), lambda item: (item, 0))
    full = pl.BlockSpec((hidden, width), lambda item: (0, 0), pipeline_mode=pl.Buffered(1))
    count = 2 if back else 3
    shape = jax.ShapeDtypeStruct
    if split:
        last_specs = specs
        last = [shape(block.shape, low) for block in blocks[:-1]] + [shape(blocks[-1].shape, wide)]
    else:
        last_specs, last = [outer], [shape((rows, width), low)]
    group, *results = pl.pallas_call(
        functools.partial(feed_back_kernel if back else feed_kernel, (len(blocks), len(last)), starts),
        grid=(tiles,),
        in_specs=specs + [inner] * len(kept) + [full] * 3,
        out_specs=[outer] + [inner] * count + last_specs,
        out_shape=[shape((rows, width), low)] + [shape((rows, hidden), low)] * count + last,
        compiler_params=pltpu.CompilerParams(vmem_limit_bytes=56 * 2**20),
        cost_estimate=pl.CostEstimate(
            flops=6 * rows * hidden * width,
            bytes_accessed=rows * (10 * hidden + 8 * width) + 6 * hidden * width,
            transcendentals=0 if back else rows * hidden,
        ),
    )(*blocks, *kept, *weights)
    return group, results[:count], results[count:] if split else results[count]


def weight_grad(lefts, rights):
    terms = [product_of(left, right, 0, 0) for left, right in zip(lefts, rights)]
    return (terms[0] + terms[1]).astype(low)


def weights_kernel(rows, place, *refs):
    blocks, outs = refs[:8], refs[8:]
    relative = pl.program_id(0) ^ place[0]
    for number, block in enumerate(blocks):

        @pl.when(relative == number)
        def _():
            for z in range(4):
                source = lax.rem(place[1] + 4 - z, 4)
                start = 0
                for out, count in zip(outs, rows):
                    out[z, 0] = block[source, start : start + count]
                    start += count


def attention_weights(shards):
    rows = [shard.shape[0] for shard in shards]
    width = shards[0].shape[1]
    shard = jnp.concatenate(shards, axis=0)
    if not by_steps():
        whole = lax.all_gather(shard, both, axis=0, tiled=False)
        starts = [sum(rows[:at]) for at in range(len(rows))]
        return [
            whole[:, start : start + count].reshape(-1, width) for start, count in zip(starts, rows)
        ]
    first, third, second = along_z(shard, 1), along_z(shard, 3), along_z(shard, 2)
    column = jnp.concatenate([shard, first, second, third], axis=0)
    far, near = group_gather(column)
    blocks = [block.reshape(4, -1, width) for at in (3, 2, 1, 0) for block in (near[at], far[at])]
    dp, seq = lax.axis_index("dp"), lax.axis_index("seq")
    place = jnp.stack([(dp % 2) * 4 + seq, dp // 2]).astype(jnp.int32)
    results = pl.pallas_call(
        functools.partial(weights_kernel, rows),
        grid=(8,),
        in_specs=[pl.BlockSpec(memory_space=pltpu.SMEM)]
        + [pl.BlockSpec((4, sum(rows), width), lambda item: (0, 0, 0), pipeline_mode=pl.Buffered(1))] * 8,
        out_specs=[pl.BlockSpec((4, 1, count, width), lambda item: (0, item, 0, 0)) for count in rows],
        out_shape=[jax.ShapeDtypeStruct((4, 8, count, width), shard.dtype) for count in rows],
        compiler_params=pltpu.CompilerParams(vmem_limit_bytes=24 * 2**20),
        cost_estimate=pl.CostEstimate(
            flops=0, bytes_accessed=64 * sum(rows) * width * 2, transcendentals=0
        ),
    )(place, *blocks)
    return [result.reshape(-1, width) for result in results]


def allowed_pairs(base, row_seg, column_seg, length, before):
    shape = (before + length, length)
    key = lax.broadcasted_iota(jnp.int32, shape, 0)
    distance = lax.broadcasted_iota(jnp.int32, shape, 1) + before - key
    allowed = (distance >= 0) & (distance < WINDOW) & (key >= before - base)
    return allowed & (column_seg == row_seg)


def shaped_query(projected, gain, cosine, sine):
    unit, scale = rms_parts(projected)
    return unit, scale, rotate(unit * (1.0 + gain), cosine, sine).astype(low)


def attend_kernel(heads, base, proj, cosine, sine, gain, own_seg, key_seg, *refs):
    *blocks, mixed, logs = refs
    length, size = cosine.shape
    keys = jnp.concatenate([block[0] for block in blocks], axis=0)
    only, values = keys[:, :size], keys[:, size:]
    before = keys.shape[0] - length
    allowed = allowed_pairs(base[0], own_seg[0], key_seg[0], length, before)
    for head in range(heads):
        at = slice(head * size, (head + 1) * size)
        _, _, query = shaped_query(proj[:, at], gain[...], cosine[...], sine[...])
        scores = product_of(only, query, 1, 1) * size**-0.5
        scores = jnp.where(allowed, scores, -1e30)
        highest = jnp.max(scores, axis=0, keepdims=True)
        expo = jnp.exp(scores - highest)
        total = jnp.sum(expo, axis=0, keepdims=True)
        probs = (expo * (1.0 / total)).astype(low)
        mixed[:, at] = product_of(probs.T, values, 1, 0).astype(low)
        logs[0, head : head + 1, :] = highest + jnp.log(total)


def attend_back_kernel(heads, base, proj, cosine, sine, gain, own_seg, key_seg, logs, grad, *refs):
    hops = (len(refs) - 3) // 2
    blocks, outs = refs[: hops + 1], refs[hops + 1 :]
    grad_proj, grad_gain = outs[0], outs[1]
    length, size = cosine.shape
    keys = jnp.concatenate([block[0] for block in blocks], axis=0)
    only, values = keys[:, :size], keys[:, size:]
    before = hops * length
    allowed = allowed_pairs(base[0], own_seg[0], key_seg[0], length, before)
    grad_keys = jnp.zeros((before + length, size), wide)
    grad_values = jnp.zeros((before + length, size), wide)
    gains = jnp.zeros((1, size), wide)
    for head in range(heads):
        at = slice(head * size, (head + 1) * size)
        unit, scale, query = shaped_query(proj[:, at], gain[...], cosine[...], sine[...])
        mixed_grad = grad[:, at]
        scores = product_of(only, query, 1, 1) * size**-0.5
        probs = jnp.where(allowed, jnp.exp(scores - logs[0, head : head + 1, :]), 0.0)
        grad_probs = product_of(values, mixed_grad, 1, 1)
        delta = jnp.sum(probs * grad_probs, axis=0, keepdims=True)
        grad_scores = (probs * (grad_probs - delta)).astype(low)
        grad_values += product_of(probs.astype(low), mixed_grad, 1, 0)
        grad_keys += product_of(grad_scores, query, 1, 0)
        grad_query = product_of(grad_scores.T, only, 1, 0) * size**-0.5
        turned = rotate_back(grad_query, cosine[...], sine[...])
        weighted = turned * (1.0 + gain[...])
        inner = jnp.mean(unit * weighted, axis=-1, keepdims=True)
        grad_proj[:, at] = (scale * (weighted - unit * inner)).astype(low)
        gains += jnp.sum(unit * turned, axis=0, keepdims=True)
    grad_gain[0] = gains
    for hop in range(hops + 1):
        rows = slice(hop * length, (hop + 1) * length)
        target = outs[2 + hop]
        target[0, :, :size] = (grad_keys[rows] * size**-0.5).astype(target.dtype)
        target[0, :, size:] = grad_values[rows].astype(target.dtype)


def attention(back, micro, length, base, projected, tables, gain, segments, key_seg, blocks, extra=()):
    size = gain.shape[-1]
    hops = len(blocks) - 1
    whole = lambda *shape: pl.BlockSpec(shape, lambda item: (0,) * len(shape))
    each = lambda *shape: pl.BlockSpec((1, *shape), lambda item: (item, 0, 0))
    flat = pl.BlockSpec((length, HEADS * size), lambda item: (item, 0))
    key_count = (hops + 1) * length
    in_specs = [
        pl.BlockSpec(memory_space=pltpu.SMEM),
        flat,
        whole(length, size),
        whole(length, size),
        whole(1, size),
        each(1, length),
        each(key_count, 1),
    ]
    logs_spec, block_spec = each(HEADS, length), each(length, 2 * size)
    shape = jax.ShapeDtypeStruct
    rows = (micro * length, HEADS * size)
    if back:
        in_specs += [logs_spec, flat]
        out_specs = [flat, each(1, size)] + [block_spec] * (hops + 1)
        out_shape = [shape(rows, low), shape((micro, 1, size), wide)]
        out_shape += [shape((micro, length, 2 * size), low)] * hops
        out_shape += [shape((micro, length, 2 * size), wide)]
    else:
        out_specs = [flat, logs_spec]
        out_shape = [shape(rows, low), shape((micro, HEADS, length), wide)]
    flops = micro * HEADS * key_count * length * size * 2 * (5 if back else 2)
    return pl.pallas_call(
        functools.partial(attend_back_kernel if back else attend_kernel, HEADS),
        grid=(micro,),
        in_specs=in_specs + [block_spec] * (hops + 1),
        out_specs=out_specs,
        out_shape=out_shape,
        compiler_params=pltpu.CompilerParams(vmem_limit_bytes=40 * 2**20),
        cost_estimate=pl.CostEstimate(
            flops=flops, bytes_accessed=10 * 2**20, transcendentals=micro * HEADS * key_count * length
        ),
    )(
        base.reshape(1),
        projected,
        *tables,
        gain.reshape(1, size),
        segments.reshape(micro, 1, length),
        key_seg.reshape(micro, key_count, 1),
        *extra,
        *blocks,
    )


def on_device(
    inputs,
    segments,
    query_weight,
    key_weight,
    value_weight,
    out_weight,
    gate_weight,
    up_weight,
    down_weight,
    input_gain,
    attention_gain,
    feed_gain,
    output_gain,
    query_gain,
    key_gain,
    cotangent,
):
    micro, length, width = inputs.shape
    rows = micro * length
    size = query_gain.shape[0]
    seq_count = lax.axis_size("seq")
    dp_count = lax.axis_size("dp")
    hops = min((WINDOW + length - 2) // length, seq_count - 1)
    seq_index = lax.axis_index("seq")
    nq, nk, nv = query_weight.shape[1], key_weight.shape[1], value_weight.shape[1]

    full_query, full_key, full_value, full_out = attention_weights(
        [query_weight.T, key_weight.T, value_weight.T, out_weight]
    )
    units = gate_weight.shape[1]
    shards = 4 if by_steps() else dp_count
    padding = next(extra for extra in range(129) if (units + extra) * shards % 128 == 0)
    padded = lambda shard: jnp.pad(shard, ((0, padding), (0, 0)))
    gate_all = hidden_gather(padded(gate_weight.T))
    up_all = hidden_gather(padded(up_weight.T))
    down_all = hidden_gather(padded(down_weight))

    positions = seq_index * length + jnp.arange(length, dtype=jnp.int32)
    cosine, sine = rope_tables(positions, size)
    source = inputs.reshape(rows, width).astype(wide)
    source_unit, source_scale = rms_parts(source)
    normed = (source_unit * (1.0 + input_gain)).astype(low)
    key_proj = product_of(normed, full_key, 1, 1).reshape(micro, length, size)
    value_low = product_of(normed, full_value, 1, 1).astype(low).reshape(micro, length, size)
    key_unit, key_scale = rms_parts(key_proj)
    key_low = rotate(key_unit * (1.0 + key_gain), cosine, sine).astype(low)
    own_block = jnp.concatenate([key_low, value_low], axis=-1)
    blocks = [own_block]
    seg_blocks = [segments]
    for hop in range(1, hops + 1):
        blocks.insert(0, passed_along(own_block, "seq", hop))
        seg_blocks.insert(0, passed_along(segments, "seq", hop))
    key_seg = jnp.concatenate(seg_blocks, axis=1)
    query_proj = product_of(normed, full_query, 1, 1)
    base = seq_index * length
    attend = functools.partial(
        attention,
        micro=micro,
        length=length,
        base=base,
        projected=query_proj,
        tables=(cosine, sine),
        gain=query_gain,
        segments=segments,
        key_seg=key_seg,
        blocks=blocks,
    )
    mixed_flat, logs = attend(back=False)
    attended = product_of(mixed_flat, full_out, 1, 0)
    attended_unit, attended_scale = rms_parts(attended)
    hidden = source + attended_unit * (1.0 + attention_gain)
    hidden_unit, hidden_scale = rms_parts(hidden)
    prenorm = (hidden_unit * (1.0 + feed_gain)).astype(low)

    weights = (gate_all, up_all, down_all)
    far, near = group_gather(prenorm)
    far, far_kept, sent = feed(False, far, (), weights, False)
    near, near_kept, kept = feed(False, near, (), weights, True)
    down, _, _ = group_reduce(sent, kept)
    flat_cotangent = cotangent.reshape(rows, width)
    output, grad_down, grad_output_gain = by_rows(
        turn_kernel, (*down, hidden, flat_cotangent), (output_gain,), (low, low), 1
    )

    grad_far, grad_near = group_gather(grad_down)
    grad_far, (far_gate, far_up), sent = feed(True, grad_far, far_kept[1:], weights, False)
    grad_near, (near_gate, near_up), kept = feed(True, grad_near, near_kept[1:], weights, True)

    def down_weight_grad(ready):
        left, _ = tied(near_kept[0], ready)
        return weight_grad((far_kept[0], left), (grad_far, grad_near))

    def gate_weight_grad(ready):
        left, _ = tied(near_gate, ready)
        return weight_grad((far_gate, left), (far, near))

    def up_weight_grad(ready):
        left, _ = tied(near_up, ready)
        return weight_grad((far_up, left), (far, near))

    grad_prenorm, grad_down_weight, (grad_gate_weight, grad_up_weight) = group_reduce(
        sent, kept, down_weight_grad, (gate_weight_grad, up_weight_grad)
    )
    shard_down = hidden_reduce(grad_down_weight)[:units]
    shard_gate = hidden_reduce(grad_gate_weight)[:units]
    shard_up = hidden_reduce(grad_up_weight)[:units]

    grad_hidden, grad_attended, gains = by_rows(
        hidden_kernel,
        (*grad_prenorm, hidden, attended, flat_cotangent),
        (feed_gain, attention_gain),
        (wide, low),
        2,
    )
    grad_feed_gain, grad_attention_gain = gains[0], gains[1]
    grad_out = product_of(mixed_flat, grad_attended, 0, 0).astype(low)
    grad_mixed = product_of(grad_attended, full_out, 1, 1).astype(low)
    grad_mixed, grad_out = tied(grad_mixed, grad_out)
    count = dp_count * seq_count
    places = (4, 2, 2, 2) if by_steps() else (count,)
    grad_out = grad_out.reshape(*places, -1, width)
    if by_steps():
        grad_out = reduce_step(grad_out, ["z", "x", "y", "core"], "core")
    grad_query_proj, query_gains, *key_grads = attend(back=True, extra=(logs, grad_mixed))
    key_grads[hops], grad_out = tied(key_grads[hops], grad_out)
    grad_query_gain = jnp.sum(query_gains, axis=(0, 1))
    grad_query = product_of(grad_query_proj, normed, 0, 0).astype(low).reshape(*places, nq, width)
    if by_steps():
        grad_out = reduce_step(grad_out, ["z", "x", "y"], "x")
        grad_query = reduce_step(grad_query, ["z", "x", "y", "core"], "core")
    returning = key_grads[hops]
    for hop in range(1, hops + 1):
        returning = returning + passed_along(key_grads[hops - hop], "seq", -hop).astype(wide)
    if by_steps():
        grad_query = reduce_step(grad_query, ["z", "x", "y"], "x")
    returning, grad_out, grad_query = tied(returning, grad_out, grad_query)
    if by_steps():
        grad_out = reduce_step(grad_out, ["z", "y"], "y")
    grad_key_proj, grad_key_gain = rms_back(
        key_unit, key_scale, key_gain, rotate_back(returning[..., :size], cosine, sine)
    )
    grad_key = grad_key_proj.astype(low).reshape(rows, size)
    grad_value = returning[..., size:].astype(low).reshape(rows, size)
    grad_kv = [
        product_of(grad, normed, 0, 0).astype(low).reshape(*places, -1, width)
        for grad in (grad_key, grad_value)
    ]
    grad_normed = product_of(grad_query_proj, full_query, 1, 0) + product_of(grad_key, full_key, 1, 0)
    grad_normed = grad_normed + product_of(grad_value, full_value, 1, 0)
    grad_source, grad_input_gain = rms_back(source_unit, source_scale, input_gain, grad_normed)
    grad_inputs = grad_hidden + grad_source

    grad_kv = jnp.concatenate(grad_kv, axis=-2)
    gains = jnp.concatenate(
        [
            grad_input_gain,
            grad_attention_gain,
            grad_feed_gain,
            grad_output_gain[0],
            grad_query_gain,
            grad_key_gain,
        ]
    )
    shard_gate = shard_gate.T
    if by_steps():
        grad_kv = reduce_step(grad_kv, ["z", "x", "y", "core"], "core")
        grad_kv, gains = tied(grad_kv, gains)
        grad_kv = reduce_step(grad_kv, ["z", "x", "y"], "x")
        joined = reduce_step(jnp.concatenate([grad_query, grad_kv], axis=-2), ["z", "y"], "y")
        joined, shard_down, shard_gate = tied(joined, shard_down, shard_gate)
        shard = reduce_z(jnp.concatenate([joined, grad_out], axis=-2))
    else:
        shard = jnp.concatenate([grad_query, grad_kv, grad_out], axis=-2)
        shard = lax.psum_scatter(shard, both, scatter_dimension=0, tiled=False).astype(wide)
    gains = sum_everywhere(gains)
    ends = (nq, nq + nk, nq + nk + nv)
    return (
        output.reshape(micro, length, width),
        grad_inputs.reshape(micro, length, width),
        shard[: ends[0]].T,
        shard[ends[0] : ends[1]].T,
        shard[ends[1] : ends[2]].T,
        shard[ends[2] :],
        shard_gate,
        shard_up.T,
        shard_down,
        gains[:width],
        gains[width : 2 * width],
        gains[2 * width : 3 * width],
        gains[3 * width : 4 * width],
        gains[4 * width : 4 * width + size],
        gains[4 * width + size :],
    )


def solution(mesh):
    in_specs = (
        P("dp", "seq", None),
        P("dp", "seq"),
        P(None, ("dp", "seq")),
        P(None, ("dp", "seq")),
        P(None, ("dp", "seq")),
        P(("dp", "seq"), None),
        P(None, ("dp", "seq")),
        P(None, ("dp", "seq")),
        P(("dp", "seq"), None),
        P(),
        P(),
        P(),
        P(),
        P(),
        P(),
        P("dp", "seq", None),
    )
    out_specs = (
        P("dp", "seq", None),
        P("dp", "seq", None),
        P(None, ("dp", "seq")),
        P(None, ("dp", "seq")),
        P(None, ("dp", "seq")),
        P(("dp", "seq"), None),
        P(None, ("dp", "seq")),
        P(None, ("dp", "seq")),
        P(("dp", "seq"), None),
        P(),
        P(),
        P(),
        P(),
        P(),
        P(),
    )
    return jax.shard_map(
        on_device, mesh=mesh, in_specs=in_specs, out_specs=out_specs, check_vma=False
    )
```
